256 devices in a mesh: seg: 4 (over x_lo, core), chan: 64 (over y, z, x_hi).
Axes of the slice: x: 4 (x_hi: 2, x_lo: 2; x = x_hi * 2 + x_lo), y: 4, z: 8, core: 2. Of those that a mesh axis runs over, the one named last changes fastest.
Arguments:
- spectra: float32 [4, 4, 8192, 1024], P('seg', None, 'chan'), may hold values from -6 to 6
- valid: int32 [4, 8192], P('seg', 'chan'), may hold values from 1 to 4
Outputs:
- stacked: float32 [2, 64, 128, 101, 128], P(None, 'chan', 'seg')
The draws below stay inside these ranges and needn't reach their ends.
All inputs are finite; a program needn't handle non-finite values.
Results may differ from the reference program's by a relative error of at most 0.019.
Values may be sent and summed in bfloat16 or wider, within the bound.
A program may use at most 192 MiB of HBM per device.

```python
import math
import jax
import jax.numpy as jnp
from jax import lax

CB = 128
F = 512
WIN = 4
SEG_DEV = 1
ROUNDS = 2
LAGS = 101
SEGMENTS = 4
CHANNELS = 8192
N_SEG = 4
N_CHAN = 64


def with_ends(result, own_key, low, top_value):
    longest = result.shape.index(max(result.shape))
    spots = []
    for shift in (0, 1):
        where = [jax.random.randint(jax.random.fold_in(own_key, axis), (), 0, length) for axis, length in enumerate(result.shape)]
        where[longest] = (where[longest] + shift) % result.shape[longest]
        spots.append(tuple(where))
    return result.at[spots[0]].set(low).at[spots[1]].set(top_value)


def levels(key, extent, cuts, low, high):
    factor_of = 1.0
    for dim, shards_of in cuts:
        draws = jax.random.uniform(jax.random.fold_in(jax.random.fold_in(key, 6), dim), (shards_of,), jnp.float32, low / len(cuts), high / len(cuts))
        factor_of = factor_of * jnp.repeat(jnp.exp(draws), extent[dim] // shards_of).reshape((-1,) + (1,) * (len(extent) - 1 - dim))
    return factor_of


def bell_draw(rng, shape, spread, most, shards=(), kind=jnp.bfloat16):
    result = spread * jax.random.normal(rng, shape, jnp.float32)
    if shards:
        result = result * levels(rng, shape, shards, -0.22, 0.18)
    return jnp.clip(result, -most, most).astype(kind)


def setup_inputs(seed: int = 0) -> dict:
    arg_keys = jax.random.split(jax.random.key(seed), 3)
    return {
        "spectra": bell_draw(arg_keys[0], (SEGMENTS, WIN, CHANNELS, 2 * F), 1.0, 6.0, ((0, 4), (2, 64)), jnp.float32),
        "valid": with_ends(jax.random.randint(arg_keys[1], (SEGMENTS, CHANNELS), 1, WIN + 1), jax.random.fold_in(arg_keys[1], 1), 1, WIN).astype(jnp.int32),
    }


def lag_table(freqs, lags):
    freq_ids = jnp.arange(freqs, dtype=jnp.int32)[:, None]
    lag_ids = jnp.arange(lags, dtype=jnp.int32)[None, :] - (lags - 1) // 2
    phase = jnp.mod(freq_ids * lag_ids, 2 * freqs).astype(jnp.float32) * (math.pi / freqs)
    return jnp.concatenate([jnp.cos(phase), -jnp.sin(phase)], 0).astype(jnp.bfloat16)

def correlate(own_rows, far_rows, table):
    half = own_rows.shape[-1] // 2
    own_real, own_imag = (own_rows[..., :half], own_rows[..., half:])
    far_real, far_imag = (far_rows[..., :half], far_rows[..., half:])

    def product(former, latter):
        return jnp.einsum('swif,swjf->ifj', former, latter, precision=lax.Precision.HIGHEST)
    real_part = product(own_real, far_real) + product(own_imag, far_imag)
    imag_part = product(own_imag, far_real) - product(own_real, far_imag)
    spectrum = jnp.concatenate([real_part, imag_part], 1).astype(jnp.bfloat16)
    return jnp.einsum('ikj,kl->ilj', spectrum.astype(jnp.float32), table.astype(jnp.float32))

def reference(spectra, valid):
    window_ids = jnp.arange(WIN, dtype=jnp.int32)[None, :, None]
    counts = valid.astype(jnp.float32)
    weight = (window_ids < valid[:, None, :]).astype(jnp.float32) / jnp.sqrt(counts)[:, None, :]
    weighted = spectra * weight[..., None]
    blocks = weighted.reshape(SEGMENTS, WIN, N_CHAN, CB, 2 * F)
    table = lag_table(F, LAGS)
    scale = 1.0 / math.sqrt(F * SEGMENTS)

    def one_pair(pair_index):
        turn_index = pair_index // N_CHAN
        block_index = pair_index % N_CHAN
        partner_index = (block_index + turn_index + 1) % N_CHAN
        own_rows = lax.dynamic_index_in_dim(blocks, block_index, 2, keepdims=False)
        far_rows = lax.dynamic_index_in_dim(blocks, partner_index, 2, keepdims=False)
        total = jnp.zeros((CB, LAGS, CB), jnp.float32)
        for group in range(N_SEG):
            first = group * SEG_DEV
            term = correlate(own_rows[first:first + SEG_DEV], far_rows[first:first + SEG_DEV], table) * scale
            rounded = lax.optimization_barrier(term.astype(jnp.bfloat16))
            total = total + rounded.astype(jnp.float32)
        return total
    pairs = lax.map(one_pair, jnp.arange(ROUNDS * N_CHAN, dtype=jnp.int32))
    return pairs.reshape(ROUNDS, N_CHAN, CB, LAGS, CB)
```

```python
import functools
import math

import jax
import jax.numpy as jnp
import ml_dtypes
import numpy as np
from jax import lax
from jax.experimental import pallas as pl
from jax.experimental.pallas import tpu as pltpu
from jax.sharding import PartitionSpec as P

MESH = pl.DeviceIdType.MESH
ROUNDS = 2
LAGS = 101
LAG_ROWS = 112
SEGS = 4
WIN = 4
CB = 128
F = 512
HALF_F = F // 2
GROUPS = HALF_F // 8
PER_STEP = 2
STEPS = GROUPS // PER_STEP
BURST = 8
ROWS = CB // 2
OUT_ROWS = CB // SEGS
AHEAD = 2
LAG_F2 = 2
LAG_F1 = 4
LAG_C = 5
PIECES = 4


def lag_table(core):
    f = core * HALF_F + np.arange(HALF_F, dtype=np.int64).reshape(GROUPS, 1, 8)
    t = np.arange(LAGS, dtype=np.int64).reshape(LAGS, 1, 1, 1) - (LAGS - 1) // 2
    phase = np.mod(f * t, 2 * F) * (math.pi / F)
    both = np.concatenate([np.cos(phase), -np.sin(phase)], 2).reshape(LAGS, GROUPS * 16)
    return np.pad(both, ((0, LAG_ROWS - LAGS), (0, 0)))


def shortcut(step):
    return lax.rem(step, 3) == 1


def kernel(n_chan, spectra, valid, table, out, staged, own, far, other, turned, left, cross, acc, sums, landed,
           in_sem, s_own, r_own, s_z, r_z, s_x, r_x, s_fz, r_fz, s_fx, r_fx, s_sum, r_sum):
    seg = lax.axis_index("seg")
    chan = lax.axis_index("chan")
    core = lax.rem(seg, 2)
    x_lo = seg // 2
    x_hi = lax.rem(chan, 2)
    sibling = (seg + 1 - 2 * core, chan)
    pair_near = (lax.rem(seg + 2, SEGS), chan)
    pair_cross = (SEGS - 1 - seg, chan)
    below = (seg, lax.rem(chan + n_chan - 2, n_chan))
    above = (seg, lax.rem(chan + 2, n_chan))
    across = (lax.rem(seg + 2, SEGS), chan + 1 - 2 * x_hi)
    near0 = 2 * x_lo
    away0 = 2 - near0

    barrier = pltpu.get_barrier_semaphore()
    for device in (sibling, pair_near, pair_cross, above, across):
        pl.semaphore_signal(barrier, inc=1, device_id=device, device_id_type=MESH)

    def load(block):
        half = lax.rem(core + block // 2, 2)
        first = half * HALF_F + lax.rem(block, 2) * 128
        copies = []
        for part in range(2):
            source = pl.multiple_of(first + part * F, 128)
            copies.append(pltpu.make_async_copy(
                spectra.at[0, :, :, pl.ds(source, 128)],
                staged.at[block, part],
                in_sem.at[block, part],
            ))
        return copies

    for block in (0, 2, 1, 3):
        for copy in load(block):
            copy.start()

    counts = valid[...]
    inverse = 1.0 / jnp.sqrt(counts.astype(jnp.float32))
    weights = [jnp.where(w < counts, inverse, 0.0) for w in range(WIN)]

    def prepare(block):
        for copy in load(block):
            copy.wait()
        for part in range(2):
            for pair in range(2):
                rows = [
                    (staged[block, part, 2 * pair + k].T * weights[2 * pair + k]).reshape(16, 8, CB)
                    for k in range(2)
                ]
                both = jnp.concatenate(rows, 1).astype(jnp.bfloat16)
                groups = pl.ds(16 * (block % 2), 16)
                place = pl.ds(part * 32 + pair * 16, 16)
                if block < 2:
                    own[seg, groups, place, :] = both
                else:
                    other[groups, place, :] = both

    def groups_of(step):
        return pl.ds(step * PER_STEP, PER_STEP)

    def own_copies(step):
        g = groups_of(step)
        mine = own.at[seg, g]
        theirs = other.at[g]
        target = own.at[seg, g]
        return [
            pltpu.make_async_remote_copy(mine, target, s_own.at[0, step], r_own.at[0, step], pair_near, MESH),
            pltpu.make_async_remote_copy(theirs, target, s_own.at[1, step], r_own.at[1, step], pair_cross, MESH),
            pltpu.make_async_remote_copy(theirs, target, s_own.at[2, step], r_own.at[2, step], sibling, MESH),
        ]

    def z_copy(step, short):
        segs = pl.ds(near0, 2) if short else pl.ds(0, SEGS)
        g = groups_of(step)
        return pltpu.make_async_remote_copy(
            own.at[segs, g], far.at[1, segs, g], s_z.at[step], r_z.at[step], below, MESH)

    def x_copy(step, short, send, from_far):
        segs = pl.ds(near0 if send else away0, 2) if short else pl.ds(0, SEGS)
        g = groups_of(step)
        source = far.at[1, segs, g] if from_far else own.at[segs, g]
        return pltpu.make_async_remote_copy(
            source, far.at[0, segs, g], s_x.at[step], r_x.at[step], across, MESH)

    def fz_copy(step, send):
        segs = pl.ds(near0 if send else away0, 2)
        piece = far.at[1, segs, groups_of(step)]
        return pltpu.make_async_remote_copy(piece, piece, s_fz.at[step], r_fz.at[step], pair_near, MESH)

    def fx_copy(step, send):
        segs = pl.ds(away0 if send else near0, 2)
        piece = far.at[0, segs, groups_of(step)]
        return pltpu.make_async_remote_copy(piece, piece, s_fx.at[step], r_fx.at[step], pair_near, MESH)

    def by_kind(step, act):
        short = shortcut(step)

        @pl.when(short)
        def _():
            act(True)

        @pl.when(jnp.logical_not(short))
        def _():
            act(False)

    def send_own(step):
        for copy in own_copies(step):
            copy.start()

    def stage_own(step):
        for copy in own_copies(step):
            copy.wait_recv()

        def act(short):
            z_copy(step, short).start()

            @pl.when(x_hi == 1)
            def _():
                x_copy(step, short, True, False).start()

        by_kind(step, act)

    def stage_z(step):
        def act(short):
            z_copy(step, short).wait_recv()

            @pl.when(x_hi == 0)
            def _():
                x_copy(step, short, True, True).start()

            if short:
                fz_copy(step, True).start()

        by_kind(step, act)

    def stage_x(step):
        def act(short):
            x_copy(step, short, False, False).wait_recv()
            if short:
                fx_copy(step, True).start()

        by_kind(step, act)

    lane = lax.broadcasted_iota(jnp.int32, (8, 128), 1)
    row = lax.broadcasted_iota(jnp.int32, (8, 128), 0)
    mask = (lax.rem(lane, 8) == row).astype(jnp.float32)
    base = x_lo * ROWS

    def spectrum(step):
        for k in range(PER_STEP):
            group = step * PER_STEP + k
            for part in range(2):
                rows = pl.ds(part * 32, 32)
                picked = jnp.concatenate([own[s, group, rows, :] for s in range(SEGS)], 0)
                turned[part] = picked.astype(jnp.float32).T
            for i in range(ROWS):
                u = turned[0, pl.ds(base + i, 1), :] * mask
                v = turned[1, pl.ds(base + i, 1), :] * mask
                left[pl.ds(i * 16, 16), 0:128] = jnp.concatenate([u, v], 0).astype(jnp.bfloat16)
                left[pl.ds(i * 16, 16), 128:256] = jnp.concatenate([v, -u], 0).astype(jnp.bfloat16)
            right = jnp.concatenate(
                [
                    jnp.concatenate(
                        [far[r, s, group, pl.ds(part * 32, 32), :] for part in range(2) for s in range(SEGS)], 0
                    )
                    for r in range(ROUNDS)
                ],
                1,
            )
            product = jnp.dot(left[...], right, preferred_element_type=jnp.float32)
            spot = pl.multiple_of(lax.rem(group, BURST) * 16, 16)
            cross[:, pl.ds(spot, 16), :] = product.reshape(ROWS, 16, ROUNDS * CB).astype(jnp.bfloat16)

    def projected(burst, i):
        columns = pl.ds(pl.multiple_of(burst * BURST * 16, BURST * 16), BURST * 16)
        return jnp.dot(table[core, :, columns], cross[i], preferred_element_type=jnp.float32)

    def stage_compute(step):
        @pl.when(shortcut(step))
        def _():
            fz_copy(step, False).wait_recv()
            fx_copy(step, False).wait_recv()

        spectrum(step)
        burst = step // (BURST // PER_STEP)

        @pl.when(jnp.logical_and(lax.rem(step, BURST // PER_STEP) == BURST // PER_STEP - 1, step < STEPS - 1))
        def _():
            @pl.loop(0, ROWS)
            def _(i):
                term = projected(burst, i)

                @pl.when(burst == 0)
                def _():
                    acc[i] = term

                @pl.when(burst > 0)
                def _():
                    acc[i] = acc[i] + term

    prepare(0)
    prepare(2)
    pl.semaphore_wait(barrier, 5)
    for step in range(AHEAD):
        send_own(step)
    prepare(1)
    prepare(3)

    @pl.loop(0, STEPS + LAG_C)
    def _(t):
        @pl.when(t + AHEAD < STEPS)
        def _():
            send_own(t + AHEAD)

        @pl.when(t < STEPS)
        def _():
            stage_own(t)

        @pl.when(jnp.logical_and(t >= LAG_F2, t < STEPS + LAG_F2))
        def _():
            stage_z(t - LAG_F2)

        @pl.when(jnp.logical_and(t >= LAG_F1, t < STEPS + LAG_F1))
        def _():
            stage_x(t - LAG_F1)

        @pl.when(t >= LAG_C)
        def _():
            stage_compute(t - LAG_C)

    per_piece = OUT_ROWS // PIECES
    last = GROUPS // BURST - 1

    def sum_copy(piece):
        rows = pl.ds(piece * per_piece, per_piece)
        return pltpu.make_async_remote_copy(
            sums.at[rows], landed.at[rows], s_sum.at[piece], r_sum.at[piece], sibling, MESH)

    for piece in range(PIECES):
        @pl.loop(0, per_piece)
        def _(k):
            q = piece * per_piece + k
            i = (1 - core) * OUT_ROWS + q
            sums[q] = (acc[i] + projected(last, i)).astype(jnp.bfloat16)

        sum_copy(piece).start()

    scale = 1.0 / math.sqrt(F * SEGS)
    for piece in range(PIECES):
        @pl.loop(0, per_piece)
        def _(k):
            i = core * OUT_ROWS + piece * per_piece + k
            acc[i] = acc[i] + projected(last, i)

    for piece in range(PIECES):
        sum_copy(piece).wait_recv()

        @pl.loop(0, per_piece)
        def _(k):
            q = piece * per_piece + k
            i = core * OUT_ROWS + q
            total = (acc[i] + landed[q].astype(jnp.float32)) * scale
            for r in range(ROUNDS):
                out[r, q] = total[:LAGS, r * CB:(r + 1) * CB]

    @pl.loop(0, STEPS)
    def _(step):
        for copy in own_copies(step):
            copy.wait_send()

        def act(short):
            z_copy(step, short).wait_send()
            x_copy(step, short, True, False).wait_send()
            if short:
                fz_copy(step, True).wait_send()
                fx_copy(step, True).wait_send()

        by_kind(step, act)

    for piece in range(PIECES):
        sum_copy(piece).wait_send()


def local(n_chan, table, spectra, valid):
    stacked = pl.pallas_call(
        functools.partial(kernel, n_chan),
        name="correlate",
        out_shape=jax.ShapeDtypeStruct((ROUNDS, OUT_ROWS, LAGS, CB), jnp.float32),
        in_specs=[
            pl.BlockSpec(memory_space=pl.ANY),
            pl.BlockSpec(memory_space=pltpu.VMEM),
            pl.BlockSpec(memory_space=pltpu.VMEM),
        ],
        out_specs=pl.BlockSpec(memory_space=pltpu.VMEM),
        scratch_shapes=[
            pltpu.VMEM((4, 2, WIN, CB, 128), jnp.float32),
            pltpu.VMEM((SEGS, GROUPS, 64, CB), jnp.bfloat16),
            pltpu.VMEM((ROUNDS, SEGS, GROUPS, 64, CB), jnp.bfloat16),
            pltpu.VMEM((GROUPS, 64, CB), jnp.bfloat16),
            pltpu.VMEM((2, CB, 128), jnp.float32),
            pltpu.VMEM((ROWS * 16, 256), jnp.bfloat16),
            pltpu.VMEM((ROWS, BURST * 16, ROUNDS * CB), jnp.bfloat16),
            pltpu.VMEM((ROWS, LAG_ROWS, ROUNDS * CB), jnp.float32),
            pltpu.VMEM((OUT_ROWS, LAG_ROWS, ROUNDS * CB), jnp.bfloat16),
            pltpu.VMEM((OUT_ROWS, LAG_ROWS, ROUNDS * CB), jnp.bfloat16),
            pltpu.SemaphoreType.DMA((4, 2)),
            pltpu.SemaphoreType.DMA((3, STEPS)),
            pltpu.SemaphoreType.DMA((3, STEPS)),
            pltpu.SemaphoreType.DMA((STEPS,)),
            pltpu.SemaphoreType.DMA((STEPS,)),
            pltpu.SemaphoreType.DMA((STEPS,)),
            pltpu.SemaphoreType.DMA((STEPS,)),
            pltpu.SemaphoreType.DMA((STEPS,)),
            pltpu.SemaphoreType.DMA((STEPS,)),
            pltpu.SemaphoreType.DMA((STEPS,)),
            pltpu.SemaphoreType.DMA((STEPS,)),
            pltpu.SemaphoreType.DMA((PIECES,)),
            pltpu.SemaphoreType.DMA((PIECES,)),
        ],
        compiler_params=pltpu.CompilerParams(
            collective_id=0, has_side_effects=True, vmem_limit_bytes=56 * 2**20),
    )(spectra, valid, table)
    return stacked[:, None]


def solution(mesh):
    n_chan = mesh.shape["chan"]

    def run(spectra, valid):
        table = jnp.asarray(np.stack([lag_table(0), lag_table(1)]).astype(ml_dtypes.bfloat16))
        return jax.shard_map(
            functools.partial(local, n_chan, table),
            mesh=mesh,
            in_specs=(P("seg", None, "chan", None), P("seg", "chan")),
            out_specs=P(None, "chan", "seg", None, None),
            check_vma=False,
        )(spectra, valid)

    return run
```

```python
import functools
import math

import jax
import jax.numpy as jnp
import ml_dtypes
import numpy as np
from jax import lax
from jax.experimental import pallas as pl
from jax.experimental.pallas import tpu as pltpu
from jax.sharding import PartitionSpec as P

MESH = pl.DeviceIdType.MESH
ROUNDS = 2
LAGS = 101
LAG_ROWS = 112
SEGS = 4
WIN = 4
CB = 128
F = 512
HALF_F = F // 2
GROUPS = HALF_F // 8
PER_STEP = 2
STEPS = GROUPS // PER_STEP
BURST = 8
ROWS = CB // 2
OUT_ROWS = CB // SEGS
AHEAD = 2
LAG_F2 = 2
LAG_F1 = 4
LAG_C = 5
PIECES = 4
LAG_BLOCK = 56
UNROLL = 8


def lag_table(core):
    f = core * HALF_F + np.arange(HALF_F, dtype=np.int64).reshape(GROUPS, 1, 8)
    t = np.arange(LAGS, dtype=np.int64).reshape(LAGS, 1, 1, 1) - (LAGS - 1) // 2
    phase = np.mod(f * t, 2 * F) * (math.pi / F)
    both = np.concatenate([np.cos(phase), -np.sin(phase)], 2).reshape(LAGS, GROUPS * 16)
    return np.pad(both, ((0, LAG_ROWS - LAGS), (0, 0)))


def shortcut(step):
    return lax.rem(step, 3) == 1


def kernel(n_chan, spectra, valid_in, table_in, kept, landed, valid, table, staged, own, far, other, turned, left, cross, acc, sums,
           in_sem, small_sem, s_own, r_own, s_z, r_z, s_x, r_x, s_fz, r_fz, s_fx, r_fx, s_sum, r_sum):
    seg = lax.axis_index("seg")
    chan = lax.axis_index("chan")
    core = lax.rem(seg, 2)
    x_lo = seg // 2
    x_hi = lax.rem(chan, 2)
    sibling = (seg + 1 - 2 * core, chan)
    pair_near = (lax.rem(seg + 2, SEGS), chan)
    pair_cross = (SEGS - 1 - seg, chan)
    below = (seg, lax.rem(chan + n_chan - 2, n_chan))
    above = (seg, lax.rem(chan + 2, n_chan))
    across = (lax.rem(seg + 2, SEGS), chan + 1 - 2 * x_hi)
    near0 = 2 * x_lo
    away0 = 2 - near0

    barrier = pltpu.get_barrier_semaphore()
    for device in (sibling, pair_near, pair_cross, above, across):
        pl.semaphore_signal(barrier, inc=1, device_id=device, device_id_type=MESH)

    def load(block):
        half = lax.rem(core + block // 2, 2)
        first = half * HALF_F + lax.rem(block, 2) * 128
        copies = []
        for part in range(2):
            source = pl.multiple_of(first + part * F, 128)
            copies.append(pltpu.make_async_copy(
                spectra.at[0, :, :, pl.ds(source, 128)],
                staged.at[block, part],
                in_sem.at[block, part],
            ))
        return copies

    valid_copy = pltpu.make_async_copy(valid_in, valid, small_sem.at[0])
    table_copy = pltpu.make_async_copy(table_in.at[core], table, small_sem.at[1])
    valid_copy.start()
    for block in (0, 2, 1, 3):
        for copy in load(block):
            copy.start()

    table_copy.start()
    valid_copy.wait()
    counts = valid[...]
    inverse = 1.0 / jnp.sqrt(counts.astype(jnp.float32))
    weights = [jnp.where(w < counts, inverse, 0.0) for w in range(WIN)]

    def prepare(block):
        for copy in load(block):
            copy.wait()
        for part in range(2):
            for pair in range(2):
                rows = [
                    (staged[block, part, 2 * pair + k].T * weights[2 * pair + k]).reshape(16, 8, CB)
                    for k in range(2)
                ]
                both = jnp.concatenate(rows, 1).astype(jnp.bfloat16)
                groups = pl.ds(16 * (block % 2), 16)
                place = pl.ds(part * 32 + pair * 16, 16)
                if block < 2:
                    own[seg, groups, place, :] = both
                else:
                    other[groups, place, :] = both

    def groups_of(step):
        return pl.ds(step * PER_STEP, PER_STEP)

    def own_copies(step):
        g = groups_of(step)
        mine = own.at[seg, g]
        theirs = other.at[g]
        target = own.at[seg, g]
        return [
            pltpu.make_async_remote_copy(mine, target, s_own.at[0, step], r_own.at[0, step], pair_near, MESH),
            pltpu.make_async_remote_copy(theirs, target, s_own.at[1, step], r_own.at[1, step], pair_cross, MESH),
            pltpu.make_async_remote_copy(theirs, target, s_own.at[2, step], r_own.at[2, step], sibling, MESH),
        ]

    def z_copy(step, short):
        segs = pl.ds(near0, 2) if short else pl.ds(0, SEGS)
        g = groups_of(step)
        return pltpu.make_async_remote_copy(
            own.at[segs, g], far.at[1, segs, g], s_z.at[step], r_z.at[step], below, MESH)

    def x_copy(step, short, send, from_far):
        segs = pl.ds(near0 if send else away0, 2) if short else pl.ds(0, SEGS)
        g = groups_of(step)
        source = far.at[1, segs, g] if from_far else own.at[segs, g]
        return pltpu.make_async_remote_copy(
            source, far.at[0, segs, g], s_x.at[step], r_x.at[step], across, MESH)

    def fz_copy(step, send):
        segs = pl.ds(near0 if send else away0, 2)
        piece = far.at[1, segs, groups_of(step)]
        return pltpu.make_async_remote_copy(piece, piece, s_fz.at[step], r_fz.at[step], pair_near, MESH)

    def fx_copy(step, send):
        segs = pl.ds(away0 if send else near0, 2)
        piece = far.at[0, segs, groups_of(step)]
        return pltpu.make_async_remote_copy(piece, piece, s_fx.at[step], r_fx.at[step], pair_near, MESH)

    def by_kind(step, act):
        short = shortcut(step)

        @pl.when(short)
        def _():
            act(True)

        @pl.when(jnp.logical_not(short))
        def _():
            act(False)

    def send_own(step):
        for copy in own_copies(step):
            copy.start()

    def stage_own(step):
        for copy in own_copies(step):
            copy.wait_recv()

        def act(short):
            z_copy(step, short).start()

            @pl.when(x_hi == 1)
            def _():
                x_copy(step, short, True, False).start()

        by_kind(step, act)

    def stage_z(step):
        def act(short):
            z_copy(step, short).wait_recv()

            @pl.when(x_hi == 0)
            def _():
                x_copy(step, short, True, True).start()

            if short:
                fz_copy(step, True).start()

        by_kind(step, act)

    def stage_x(step):
        def act(short):
            x_copy(step, short, False, False).wait_recv()
            if short:
                fx_copy(step, True).start()

        by_kind(step, act)

    lane = lax.broadcasted_iota(jnp.int32, (8, 128), 1)
    row = lax.broadcasted_iota(jnp.int32, (8, 128), 0)
    mask = (lax.rem(lane, 8) == row).astype(jnp.float32)
    base = x_lo * ROWS

    def spectrum(step):
        for k in range(PER_STEP):
            group = step * PER_STEP + k
            for part in range(2):
                rows = pl.ds(part * 32, 32)
                picked = jnp.concatenate([own[s, group, rows, :] for s in range(SEGS)], 0)
                turned[part] = picked.astype(jnp.float32).T
            for i in range(ROWS):
                u = turned[0, pl.ds(base + i, 1), :] * mask
                v = turned[1, pl.ds(base + i, 1), :] * mask
                left[pl.ds(i * 16, 16), 0:128] = jnp.concatenate([u, v], 0).astype(jnp.bfloat16)
                left[pl.ds(i * 16, 16), 128:256] = jnp.concatenate([v, -u], 0).astype(jnp.bfloat16)
            right = jnp.concatenate(
                [
                    jnp.concatenate(
                        [far[r, s, group, pl.ds(part * 32, 32), :] for part in range(2) for s in range(SEGS)], 0
                    )
                    for r in range(ROUNDS)
                ],
                1,
            )
            product = jnp.dot(left[...], right, preferred_element_type=jnp.float32)
            spot = pl.multiple_of(lax.rem(group, BURST) * 16, 16)
            cross[:, pl.ds(spot, 16), :] = product.reshape(ROWS, 16, ROUNDS * CB).astype(jnp.bfloat16)

    def projected(burst, i):
        columns = pl.ds(pl.multiple_of(burst * BURST * 16, BURST * 16), BURST * 16)
        return jnp.dot(table[:, columns], cross[i], preferred_element_type=jnp.float32)

    def stage_compute(step):
        @pl.when(shortcut(step))
        def _():
            fz_copy(step, False).wait_recv()
            fx_copy(step, False).wait_recv()

        spectrum(step)
        burst = step // (BURST // PER_STEP)

        @pl.when(jnp.logical_and(lax.rem(step, BURST // PER_STEP) == BURST // PER_STEP - 1, step < STEPS - 1))
        def _():
            @pl.when(burst == 0)
            def _():
                @pl.loop(0, ROWS // UNROLL)
                def _(first):
                    for k in range(UNROLL):
                        i = first * UNROLL + k
                        acc[i] = projected(burst, i)

            @pl.when(burst > 0)
            def _():
                @pl.loop(0, ROWS // UNROLL)
                def _(first):
                    for k in range(UNROLL):
                        i = first * UNROLL + k
                        acc[i] = acc[i] + projected(burst, i)

    prepare(0)
    prepare(2)
    pl.semaphore_wait(barrier, 5)
    for step in range(AHEAD):
        send_own(step)
    prepare(1)
    prepare(3)
    table_copy.wait()

    @pl.loop(0, STEPS + LAG_C)
    def _(t):
        @pl.when(t + AHEAD < STEPS)
        def _():
            send_own(t + AHEAD)

        @pl.when(t < STEPS)
        def _():
            stage_own(t)

        @pl.when(jnp.logical_and(t >= LAG_F2, t < STEPS + LAG_F2))
        def _():
            stage_z(t - LAG_F2)

        @pl.when(jnp.logical_and(t >= LAG_F1, t < STEPS + LAG_F1))
        def _():
            stage_x(t - LAG_F1)

        @pl.when(t >= LAG_C)
        def _():
            stage_compute(t - LAG_C)

    per_piece = OUT_ROWS // PIECES
    last = GROUPS // BURST - 1

    def sum_copy(piece):
        rows = pl.ds(piece * per_piece, per_piece)
        return pltpu.make_async_remote_copy(
            sums.at[rows], landed.at[rows], s_sum.at[piece], r_sum.at[piece], sibling, MESH)

    for piece in range(PIECES):
        for k in range(per_piece):
            q = piece * per_piece + k
            i = (1 - core) * OUT_ROWS + q
            sums[q] = (acc[i] + projected(last, i)).astype(jnp.bfloat16)
        sum_copy(piece).start()

    @pl.loop(0, OUT_ROWS // UNROLL)
    def _(first):
        for k in range(UNROLL):
            q = first * UNROLL + k
            i = core * OUT_ROWS + q
            kept[q] = acc[i] + projected(last, i)

    for piece in range(PIECES):
        sum_copy(piece).wait_recv()

    @pl.loop(0, STEPS)
    def _(step):
        for copy in own_copies(step):
            copy.wait_send()

        def act(short):
            z_copy(step, short).wait_send()
            x_copy(step, short, True, False).wait_send()
            if short:
                fz_copy(step, True).wait_send()
                fx_copy(step, True).wait_send()

        by_kind(step, act)

    for piece in range(PIECES):
        sum_copy(piece).wait_send()


def finish(kept, landed, out):
    scale = 1.0 / math.sqrt(F * SEGS)
    lanes = pl.ds(pl.multiple_of(pl.program_id(0) * CB, CB), CB)
    lags = pl.ds(pl.multiple_of(pl.program_id(1) * LAG_BLOCK, LAG_BLOCK), LAG_BLOCK)
    for i in range(0, OUT_ROWS, 8):
        rows = pl.ds(i, 8)
        total = (kept[rows, lags, lanes] + landed[rows, lags, lanes].astype(jnp.float32)) * scale
        total = jnp.swapaxes(total, 0, 1)
        for lag in range(LAG_BLOCK):
            out[0, pl.ds(lag * OUT_ROWS + i, 8), :] = total[lag]


def local(n_chan, table, spectra, valid):
    kept, landed = pl.pallas_call(
        functools.partial(kernel, n_chan),
        name="correlate",
        out_shape=[
            pltpu.VMEM((OUT_ROWS, LAG_ROWS, ROUNDS * CB), jnp.float32),
            pltpu.VMEM((OUT_ROWS, LAG_ROWS, ROUNDS * CB), jnp.bfloat16),
        ],
        in_specs=[
            pl.BlockSpec(memory_space=pltpu.HBM),
            pl.BlockSpec(memory_space=pltpu.HBM),
            pl.BlockSpec(memory_space=pltpu.HBM),
        ],
        out_specs=[pl.BlockSpec(memory_space=pltpu.VMEM)] * 2,
        scratch_shapes=[
            pltpu.VMEM((1, CB), jnp.int32),
            pltpu.VMEM((LAG_ROWS, GROUPS * 16), jnp.bfloat16),
            pltpu.VMEM((4, 2, WIN, CB, 128), jnp.float32),
            pltpu.VMEM((SEGS, GROUPS, 64, CB), jnp.bfloat16),
            pltpu.VMEM((ROUNDS, SEGS, GROUPS, 64, CB), jnp.bfloat16),
            pltpu.VMEM((GROUPS, 64, CB), jnp.bfloat16),
            pltpu.VMEM((2, CB, 128), jnp.float32),
            pltpu.VMEM((ROWS * 16, 256), jnp.bfloat16),
            pltpu.VMEM((ROWS, BURST * 16, ROUNDS * CB), jnp.bfloat16),
            pltpu.VMEM((ROWS, LAG_ROWS, ROUNDS * CB), jnp.float32),
            pltpu.VMEM((OUT_ROWS, LAG_ROWS, ROUNDS * CB), jnp.bfloat16),
            pltpu.SemaphoreType.DMA((4, 2)),
            pltpu.SemaphoreType.DMA((2,)),
            pltpu.SemaphoreType.DMA((3, STEPS)),
            pltpu.SemaphoreType.DMA((3, STEPS)),
            pltpu.SemaphoreType.DMA((STEPS,)),
            pltpu.SemaphoreType.DMA((STEPS,)),
            pltpu.SemaphoreType.DMA((STEPS,)),
            pltpu.SemaphoreType.DMA((STEPS,)),
            pltpu.SemaphoreType.DMA((STEPS,)),
            pltpu.SemaphoreType.DMA((STEPS,)),
            pltpu.SemaphoreType.DMA((STEPS,)),
            pltpu.SemaphoreType.DMA((STEPS,)),
            pltpu.SemaphoreType.DMA((PIECES,)),
            pltpu.SemaphoreType.DMA((PIECES,)),
        ],
        compiler_params=pltpu.CompilerParams(
            collective_id=0, has_side_effects=True, vmem_limit_bytes=32 * 2**20),
    )(*(pltpu.with_memory_space_constraint(x, pltpu.HBM) for x in (spectra, valid, table)))
    whole = pl.BlockSpec(memory_space=pltpu.VMEM)
    stacked = pl.pallas_call(
        finish,
        name="finish",
        grid=(ROUNDS, LAG_ROWS // LAG_BLOCK),
        out_shape=jax.ShapeDtypeStruct((ROUNDS, LAGS * OUT_ROWS, CB), jnp.float32),
        in_specs=[whole, whole],
        out_specs=pl.BlockSpec((1, LAG_BLOCK * OUT_ROWS, CB), lambda r, l: (r, l, 0)),
        compiler_params=pltpu.CompilerParams(vmem_limit_bytes=16 * 2**20),
    )(pltpu.with_memory_space_constraint(kept, pltpu.VMEM), pltpu.with_memory_space_constraint(landed, pltpu.VMEM))
    return stacked.reshape(ROUNDS, 1, LAGS, OUT_ROWS, CB).transpose(0, 1, 3, 2, 4)


def solution(mesh):
    n_chan = mesh.shape["chan"]

    def run(spectra, valid):
        table = jnp.asarray(np.stack([lag_table(0), lag_table(1)]).astype(ml_dtypes.bfloat16))
        return jax.shard_map(
            functools.partial(local, n_chan, table),
            mesh=mesh,
            in_specs=(P("seg", None, "chan", None), P("seg", "chan")),
            out_specs=P(None, "chan", "seg", None, None),
            check_vma=False,
        )(spectra, valid)

    return run
```

```python
import functools
import math

import jax
import jax.numpy as jnp
import ml_dtypes
import numpy as np
from jax import lax
from jax.experimental import pallas as pl
from jax.experimental.pallas import tpu as pltpu
from jax.sharding import PartitionSpec as P

MESH = pl.DeviceIdType.MESH
ROUNDS = 2
LAGS = 101
LAG_ROWS = 112
SEGS = 4
WIN = 4
CB = 128
F = 512
HALF_F = F // 2
GROUPS = HALF_F // 8
PER_STEP = 2
STEPS = GROUPS // PER_STEP
BURST = 8
ROWS = CB // 2
OUT_ROWS = CB // SEGS
HALF = CB // 2
AHEAD = 2
LAG_F2 = 2
LAG_F1 = 4
LAG_C = 6
PIECES = 4
LAG_BLOCK = 56
UNROLL = 8


def lag_table(core):
    f = core * HALF_F + np.arange(HALF_F, dtype=np.int64).reshape(GROUPS, 1, 8)
    t = np.arange(LAGS, dtype=np.int64).reshape(LAGS, 1, 1, 1) - (LAGS - 1) // 2
    phase = np.mod(f * t, 2 * F) * (math.pi / F)
    both = np.concatenate([np.cos(phase), -np.sin(phase)], 2).reshape(LAGS, GROUPS * 16)
    return np.pad(both, ((0, LAG_ROWS - LAGS), (0, 0)))


def kernel(n_chan, spectra, valid_in, table_in, kept, landed, valid, table, staged, own, far, other, turned, left, cross, acc, sums,
           in_sem, small_sem, s_own, r_own, s_z, r_z, s_x, r_x, s_f, r_f, s_sum, r_sum):
    seg = lax.axis_index("seg")
    chan = lax.axis_index("chan")
    core = lax.rem(seg, 2)
    x_lo = seg // 2
    x_hi = lax.rem(chan, 2)
    sibling = (seg + 1 - 2 * core, chan)
    pair_near = (lax.rem(seg + 2, SEGS), chan)
    pair_cross = (SEGS - 1 - seg, chan)
    below = (seg, lax.rem(chan + n_chan - 2, n_chan))
    above = (seg, lax.rem(chan + 2, n_chan))
    across = (lax.rem(seg + 2, SEGS), chan + 1 - 2 * x_hi)
    near = pl.ds(2 * x_lo, 2)
    away = pl.ds(2 - 2 * x_lo, 2)

    barrier = pltpu.get_barrier_semaphore()
    for device in (sibling, pair_near, pair_cross, above, across):
        pl.semaphore_signal(barrier, inc=1, device_id=device, device_id_type=MESH)

    def load(block):
        half = lax.rem(core + block // 2, 2)
        first = half * HALF_F + lax.rem(block, 2) * 128
        copies = []
        for part in range(2):
            source = pl.multiple_of(first + part * F, 128)
            copies.append(pltpu.make_async_copy(
                spectra.at[0, :, :, pl.ds(source, 128)],
                staged.at[block, part],
                in_sem.at[block, part],
            ))
        return copies

    valid_copy = pltpu.make_async_copy(valid_in, valid, small_sem.at[0])
    table_copy = pltpu.make_async_copy(table_in.at[core], table, small_sem.at[1])
    valid_copy.start()
    for block in (0, 2, 1, 3):
        for copy in load(block):
            copy.start()

    table_copy.start()
    valid_copy.wait()
    first_half = lax.broadcasted_iota(jnp.int32, (8, 8, CB), 2) < HALF
    counts = valid[...]
    inverse = 1.0 / jnp.sqrt(counts.astype(jnp.float32))
    weights = [jnp.where(w < counts, inverse, 0.0) for w in range(WIN)]

    def prepare(block):
        for copy in load(block):
            copy.wait()
        steps = pl.ds(8 * (block % 2), 8)
        for part in range(2):
            for pair in range(2):
                lows, highs = [], []
                for w in (2 * pair, 2 * pair + 1):
                    rows = (staged[block, part, w].T * weights[w]).reshape(8, 2, 8, CB)
                    even = rows[:, 0]
                    odd = pltpu.roll(rows[:, 1].reshape(64, CB), HALF, 1).reshape(8, 8, CB)
                    lows.append(jnp.where(first_half, even, odd))
                    highs.append(jnp.where(first_half, odd, even))
                place = pl.ds(part * 32 + pair * 16, 16)
                for half, both in enumerate((lows, highs)):
                    both = jnp.concatenate(both, 1).astype(jnp.bfloat16)
                    if block < 2:
                        own[seg, steps, half, place, :] = both
                    else:
                        other[steps, half, place, :] = both

    def own_copies(step):
        half = 1 - x_lo
        target = own.at[seg, step, half]
        return [
            pltpu.make_async_remote_copy(
                own.at[seg, step, half], target, s_own.at[0, step], r_own.at[0, step], pair_near, MESH),
            pltpu.make_async_remote_copy(
                other.at[step, half], target, s_own.at[1, step], r_own.at[1, step], pair_cross, MESH),
            pltpu.make_async_remote_copy(
                other.at[step], own.at[seg, step], s_own.at[2, step], r_own.at[2, step], sibling, MESH),
        ]

    def own_arrivals(step):
        def arrival(kind, place):
            return pltpu.make_async_remote_copy(
                place, place, s_own.at[kind, step], r_own.at[kind, step], sibling, MESH)

        return [
            arrival(0, own.at[pair_near[0], step, x_lo]),
            arrival(1, own.at[pair_cross[0], step, x_lo]),
            arrival(2, own.at[sibling[0], step]),
        ]

    def z_copy(step, part):
        if part == 0:
            source, target = own.at[near, step], far.at[1, near, step]
        else:
            source, target = own.at[away, step, x_lo], far.at[1, away, step, x_lo]
        return pltpu.make_async_remote_copy(source, target, s_z.at[part, step], r_z.at[part, step], below, MESH)

    def x_copy(step, part, from_far):
        segs = near if part == 0 else away
        place = (segs, step) if part == 0 else (segs, step, x_lo)
        source = far.at[(1,) + place] if from_far else own.at[place]
        return pltpu.make_async_remote_copy(
            source, far.at[(0,) + place], s_x.at[part, step], r_x.at[part, step], across, MESH)

    def x_arrival(step, part):
        place = far.at[0, away, step] if part == 0 else far.at[0, near, step, 1 - x_lo]
        return pltpu.make_async_remote_copy(place, place, s_x.at[part, step], r_x.at[part, step], across, MESH)

    def pair_copy(step, which, send):
        if which == 1:
            place = far.at[1, near if send else away, step, x_lo if send else 1 - x_lo]
        else:
            place = far.at[0, away if send else near, step, 1 - x_lo if send else x_lo]
        return pltpu.make_async_remote_copy(place, place, s_f.at[which, step], r_f.at[which, step], pair_near, MESH)

    def send_own(step):
        for copy in own_copies(step):
            copy.start()

    def stage_own(step):
        arrivals = own_arrivals(step)
        arrivals[2].wait_recv()
        z_copy(step, 0).start()

        @pl.when(x_hi == 1)
        def _():
            x_copy(step, 0, False).start()

        arrivals[0].wait_recv()
        arrivals[1].wait_recv()
        z_copy(step, 1).start()

        @pl.when(x_hi == 1)
        def _():
            x_copy(step, 1, False).start()

    def stage_z(step):
        z_copy(step, 0).wait_recv()
        pair_copy(step, 1, True).start()

        @pl.when(x_hi == 0)
        def _():
            x_copy(step, 0, True).start()

        z_copy(step, 1).wait_recv()

        @pl.when(x_hi == 0)
        def _():
            x_copy(step, 1, True).start()

    def stage_x(step):
        x_arrival(step, 0).wait_recv()
        pair_copy(step, 0, True).start()
        x_arrival(step, 1).wait_recv()

    lane = lax.broadcasted_iota(jnp.int32, (8, 128), 1)
    row = lax.broadcasted_iota(jnp.int32, (8, 128), 0)
    low_lanes = lax.broadcasted_iota(jnp.int32, (256, CB), 1) < HALF
    mask = (lax.rem(lane, 8) == row).astype(jnp.float32)

    def spectrum(step, k):
        if k == 0:
            for part in range(2):
                rows = pl.ds(part * 32, 32)
                picked = jnp.concatenate([own[s, step, x_lo, rows, :] for s in range(SEGS)], 0)
                turned[part] = picked.astype(jnp.float32).T
        base = ROWS * lax.rem(k + x_lo, 2)
        for i in range(ROWS):
            u = turned[0, pl.ds(base + i, 1), :] * mask
            v = turned[1, pl.ds(base + i, 1), :] * mask
            left[pl.ds(i * 16, 16), 0:128] = jnp.concatenate([u, v], 0).astype(jnp.bfloat16)
            left[pl.ds(i * 16, 16), 128:256] = jnp.concatenate([v, -u], 0).astype(jnp.bfloat16)
        blocks = []
        for r in range(ROUNDS):
            low, high = [
                jnp.concatenate(
                    [far[r, s, step, half, pl.ds(part * 32, 32), :] for part in range(2) for s in range(SEGS)], 0
                ).astype(jnp.float32)
                for half in range(2)
            ]
            if k == 0:
                block = jnp.where(low_lanes, low, high)
            else:
                block = pltpu.roll(jnp.where(low_lanes, high, low), HALF, 1)
            blocks.append(block.astype(jnp.bfloat16))
        right = jnp.concatenate(blocks, 1)
        product = jnp.dot(left[...], right, preferred_element_type=jnp.float32)
        group = step * PER_STEP + k
        spot = pl.multiple_of(lax.rem(group, BURST) * 16, 16)
        slot = lax.rem(group // BURST, 2)
        cross[slot, :, pl.ds(spot, 16), :] = product.reshape(ROWS, 16, ROUNDS * CB).astype(jnp.bfloat16)

    def projected(burst, i):
        columns = pl.ds(pl.multiple_of(burst * BURST * 16, BURST * 16), BURST * 16)
        slot = burst % 2 if isinstance(burst, int) else lax.rem(burst, 2)
        return jnp.dot(table[:, columns], cross[slot, i], preferred_element_type=jnp.float32)

    per_burst = BURST // PER_STEP
    share = ROWS // per_burst

    def project_share(step):
        burst = step // per_burst - 1
        first = lax.rem(step, per_burst) * share

        @pl.when(burst == 0)
        def _():
            for k in range(share):
                acc[first + k] = projected(burst, first + k)

        @pl.when(burst > 0)
        def _():
            for k in range(share):
                acc[first + k] = acc[first + k] + projected(burst, first + k)

    prepare(0)
    prepare(2)
    pl.semaphore_wait(barrier, 5)
    for step in range(AHEAD):
        send_own(step)
    prepare(1)
    prepare(3)
    table_copy.wait()

    @pl.loop(0, STEPS + LAG_C)
    def _(t):
        @pl.when(t + AHEAD < STEPS)
        def _():
            send_own(t + AHEAD)

        @pl.when(t < STEPS)
        def _():
            stage_own(t)

        @pl.when(t >= LAG_C)
        def _():
            pair_copy(t - LAG_C, 1, False).wait_recv()
            pair_copy(t - LAG_C, 0, False).wait_recv()
            spectrum(t - LAG_C, 0)

        @pl.when(jnp.logical_and(t >= LAG_F2, t < STEPS + LAG_F2))
        def _():
            stage_z(t - LAG_F2)

        @pl.when(t >= LAG_C)
        def _():
            spectrum(t - LAG_C, 1)

        @pl.when(jnp.logical_and(t >= LAG_F1, t < STEPS + LAG_F1))
        def _():
            stage_x(t - LAG_F1)

        @pl.when(t >= LAG_C + per_burst)
        def _():
            project_share(t - LAG_C)

    per_piece = OUT_ROWS // PIECES
    last = GROUPS // BURST - 1

    def sum_copy(piece):
        rows = pl.ds(piece * per_piece, per_piece)
        return pltpu.make_async_remote_copy(
            sums.at[rows], landed.at[rows], s_sum.at[piece], r_sum.at[piece], sibling, MESH)

    for piece in range(PIECES):
        for k in range(per_piece):
            q = piece * per_piece + k
            i = (1 - core) * OUT_ROWS + q
            sums[q] = (acc[i] + projected(last, i)).astype(jnp.bfloat16)
        sum_copy(piece).start()

    @pl.loop(0, OUT_ROWS // UNROLL)
    def _(first):
        for k in range(UNROLL):
            q = first * UNROLL + k
            i = core * OUT_ROWS + q
            kept[q] = acc[i] + projected(last, i)

    for piece in range(PIECES):
        sum_copy(piece).wait_recv()

    @pl.loop(0, STEPS)
    def _(step):
        for copy in own_copies(step):
            copy.wait_send()

        for part in range(2):
            z_copy(step, part).wait_send()
            x_copy(step, part, False).wait_send()
            pair_copy(step, part, True).wait_send()

    for piece in range(PIECES):
        sum_copy(piece).wait_send()


def finish(kept, landed, out):
    scale = 1.0 / math.sqrt(F * SEGS)
    lanes = pl.ds(pl.multiple_of(pl.program_id(0) * CB, CB), CB)
    lags = pl.ds(pl.multiple_of(pl.program_id(1) * LAG_BLOCK, LAG_BLOCK), LAG_BLOCK)
    for i in range(0, OUT_ROWS, 8):
        rows = pl.ds(i, 8)
        total = (kept[rows, lags, lanes] + landed[rows, lags, lanes].astype(jnp.float32)) * scale
        total = jnp.swapaxes(total, 0, 1)
        for lag in range(LAG_BLOCK):
            out[0, pl.ds(lag * OUT_ROWS + i, 8), :] = total[lag]


def local(n_chan, table, spectra, valid):
    kept, landed = pl.pallas_call(
        functools.partial(kernel, n_chan),
        name="correlate",
        out_shape=[
            pltpu.VMEM((OUT_ROWS, LAG_ROWS, ROUNDS * CB), jnp.float32),
            pltpu.VMEM((OUT_ROWS, LAG_ROWS, ROUNDS * CB), jnp.bfloat16),
        ],
        in_specs=[
            pl.BlockSpec(memory_space=pltpu.HBM),
            pl.BlockSpec(memory_space=pltpu.HBM),
            pl.BlockSpec(memory_space=pltpu.HBM),
        ],
        out_specs=[pl.BlockSpec(memory_space=pltpu.VMEM)] * 2,
        scratch_shapes=[
            pltpu.VMEM((1, CB), jnp.int32),
            pltpu.VMEM((LAG_ROWS, GROUPS * 16), jnp.bfloat16),
            pltpu.VMEM((4, 2, WIN, CB, 128), jnp.float32),
            pltpu.VMEM((SEGS, STEPS, 2, 64, CB), jnp.bfloat16),
            pltpu.VMEM((ROUNDS, SEGS, STEPS, 2, 64, CB), jnp.bfloat16),
            pltpu.VMEM((STEPS, 2, 64, CB), jnp.bfloat16),
            pltpu.VMEM((2, CB, 128), jnp.float32),
            pltpu.VMEM((ROWS * 16, 256), jnp.bfloat16),
            pltpu.VMEM((2, ROWS, BURST * 16, ROUNDS * CB), jnp.bfloat16),
            pltpu.VMEM((ROWS, LAG_ROWS, ROUNDS * CB), jnp.float32),
            pltpu.VMEM((OUT_ROWS, LAG_ROWS, ROUNDS * CB), jnp.bfloat16),
            pltpu.SemaphoreType.DMA((4, 2)),
            pltpu.SemaphoreType.DMA((2,)),
            pltpu.SemaphoreType.DMA((3, STEPS)),
            pltpu.SemaphoreType.DMA((3, STEPS)),
            pltpu.SemaphoreType.DMA((2, STEPS)),
            pltpu.SemaphoreType.DMA((2, STEPS)),
            pltpu.SemaphoreType.DMA((2, STEPS)),
            pltpu.SemaphoreType.DMA((2, STEPS)),
            pltpu.SemaphoreType.DMA((2, STEPS)),
            pltpu.SemaphoreType.DMA((2, STEPS)),
            pltpu.SemaphoreType.DMA((PIECES,)),
            pltpu.SemaphoreType.DMA((PIECES,)),
        ],
        compiler_params=pltpu.CompilerParams(
            collective_id=0, has_side_effects=True, vmem_limit_bytes=32 * 2**20),
    )(*(pltpu.with_memory_space_constraint(x, pltpu.HBM) for x in (spectra, valid, table)))
    whole = pl.BlockSpec(memory_space=pltpu.VMEM)
    stacked = pl.pallas_call(
        finish,
        name="finish",
        grid=(ROUNDS, LAG_ROWS // LAG_BLOCK),
        out_shape=jax.ShapeDtypeStruct((ROUNDS, LAGS * OUT_ROWS, CB), jnp.float32),
        in_specs=[whole, whole],
        out_specs=pl.BlockSpec((1, LAG_BLOCK * OUT_ROWS, CB), lambda r, l: (r, l, 0)),
        compiler_params=pltpu.CompilerParams(vmem_limit_bytes=16 * 2**20),
    )(pltpu.with_memory_space_constraint(kept, pltpu.VMEM), pltpu.with_memory_space_constraint(landed, pltpu.VMEM))
    return stacked.reshape(ROUNDS, 1, LAGS, OUT_ROWS, CB).transpose(0, 1, 3, 2, 4)


def solution(mesh):
    n_chan = mesh.shape["chan"]

    def run(spectra, valid):
        table = jnp.asarray(np.stack([lag_table(0), lag_table(1)]).astype(ml_dtypes.bfloat16))
        return jax.shard_map(
            functools.partial(local, n_chan, table),
            mesh=mesh,
            in_specs=(P("seg", None, "chan", None), P("seg", "chan")),
            out_specs=P(None, "chan", "seg", None, None),
            check_vma=False,
        )(spectra, valid)

    return run
```

```python
import functools
import math

import jax
import jax.numpy as jnp
import ml_dtypes
import numpy as np
from jax import lax
from jax.experimental import pallas as pl
from jax.experimental.pallas import tpu as pltpu
from jax.sharding import PartitionSpec as P

MESH = pl.DeviceIdType.MESH
ROUNDS = 2
LAGS = 101
LAG_ROWS = 112
SEGS = 4
WIN = 4
CB = 128
F = 512
HALF_F = F // 2
GROUPS = HALF_F // 8
PER_STEP = 2
STEPS = GROUPS // PER_STEP
BURST = 8
ROWS = CB // 2
OUT_ROWS = CB // SEGS
HALF = CB // 2
AHEAD = 2
LAG_F2 = 2
LAG_F1 = 3
LAG_C = 5
Z_SIZE = 8
Z_DELAY = 1
PIECES = 4
LAG_BLOCK = 16
UNROLL = 8


def lag_table(core):
    f = core * HALF_F + np.arange(HALF_F, dtype=np.int64).reshape(GROUPS, 1, 8)
    t = np.arange(LAGS, dtype=np.int64).reshape(LAGS, 1, 1, 1) - (LAGS - 1) // 2
    phase = np.mod(f * t, 2 * F) * (math.pi / F)
    both = np.concatenate([np.cos(phase), -np.sin(phase)], 2).reshape(LAGS, GROUPS * 16)
    return np.pad(both, ((0, LAG_ROWS - LAGS), (0, 0)))


def kernel(n_chan, spectra, valid_in, table_in, kept, landed, valid, table, staged, own, far, other, turned, left, cross, acc, sums,
           in_sem, small_sem, s_own, r_own, s_z, r_z, s_x, r_x, s_f, r_f, s_sum, r_sum, z_ready):
    seg = lax.axis_index("seg")
    chan = lax.axis_index("chan")
    core = lax.rem(seg, 2)
    x_lo = seg // 2
    x_hi = lax.rem(chan, 2)
    sibling = (seg + 1 - 2 * core, chan)
    pair_near = (lax.rem(seg + 2, SEGS), chan)
    pair_cross = (SEGS - 1 - seg, chan)
    below = (seg, lax.rem(chan + n_chan - 2, n_chan))
    above = (seg, lax.rem(chan + 2, n_chan))
    across = (lax.rem(seg + 2, SEGS), chan + 1 - 2 * x_hi)
    near = pl.ds(2 * x_lo, 2)
    away = pl.ds(2 - 2 * x_lo, 2)

    barrier = pltpu.get_barrier_semaphore()
    late = lax.rem(chan // 2, Z_SIZE) == 0
    for device in (sibling, pair_near, pair_cross, below, across):
        pl.semaphore_signal(barrier, inc=1, device_id=device, device_id_type=MESH)

    def load(block):
        half = lax.rem(core + block // 2, 2)
        first = half * HALF_F + lax.rem(block, 2) * 128
        copies = []
        for part in range(2):
            source = pl.multiple_of(first + part * F, 128)
            copies.append(pltpu.make_async_copy(
                spectra.at[0, :, :, pl.ds(source, 128)],
                staged.at[block, part],
                in_sem.at[block, part],
            ))
        return copies

    valid_copy = pltpu.make_async_copy(valid_in, valid, small_sem.at[0])
    table_copy = pltpu.make_async_copy(table_in.at[core], table, small_sem.at[1])
    valid_copy.start()
    for block in (0, 2, 1, 3):
        for copy in load(block):
            copy.start()

    table_copy.start()
    valid_copy.wait()
    first_half = lax.broadcasted_iota(jnp.int32, (8, 8, CB), 2) < HALF
    counts = valid[...]
    inverse = 1.0 / jnp.sqrt(counts.astype(jnp.float32))
    weights = [jnp.where(w < counts, inverse, 0.0) for w in range(WIN)]

    def prepare(block):
        for copy in load(block):
            copy.wait()
        steps = pl.ds(8 * (block % 2), 8)
        for part in range(2):
            for pair in range(2):
                lows, highs = [], []
                for w in (2 * pair, 2 * pair + 1):
                    rows = (staged[block, part, w].T * weights[w]).reshape(8, 2, 8, CB)
                    even = rows[:, 0]
                    odd = pltpu.roll(rows[:, 1].reshape(64, CB), HALF, 1).reshape(8, 8, CB)
                    lows.append(jnp.where(first_half, even, odd))
                    highs.append(jnp.where(first_half, odd, even))
                place = pl.ds(part * 32 + pair * 16, 16)
                for half, both in enumerate((lows, highs)):
                    both = jnp.concatenate(both, 1).astype(jnp.bfloat16)
                    if block < 2:
                        own[seg, steps, half, place, :] = both
                    else:
                        other[steps, half, place, :] = both

    def own_copies(step):
        half = 1 - x_lo
        target = own.at[seg, step, half]
        return [
            pltpu.make_async_remote_copy(
                own.at[seg, step, half], target, s_own.at[0, step], r_own.at[0, step], pair_near, MESH),
            pltpu.make_async_remote_copy(
                other.at[step, half], target, s_own.at[1, step], r_own.at[1, step], pair_cross, MESH),
            pltpu.make_async_remote_copy(
                other.at[step], own.at[seg, step], s_own.at[2, step], r_own.at[2, step], sibling, MESH),
        ]

    def own_arrivals(step):
        def arrival(kind, place):
            return pltpu.make_async_remote_copy(
                place, place, s_own.at[kind, step], r_own.at[kind, step], sibling, MESH)

        return [
            arrival(0, own.at[pair_near[0], step, x_lo]),
            arrival(1, own.at[pair_cross[0], step, x_lo]),
            arrival(2, own.at[sibling[0], step]),
        ]

    def z_copy(step, part):
        if part == 0:
            source, target = own.at[near, step], far.at[1, near, step]
        else:
            source, target = own.at[away, step, x_lo], far.at[1, away, step, x_lo]
        return pltpu.make_async_remote_copy(source, target, s_z.at[part, step], r_z.at[part, step], below, MESH)

    def x_copy(step, part, from_far):
        segs = near if part == 0 else away
        place = (segs, step) if part == 0 else (segs, step, x_lo)
        source = far.at[(1,) + place] if from_far else own.at[place]
        return pltpu.make_async_remote_copy(
            source, far.at[(0,) + place], s_x.at[part, step], r_x.at[part, step], across, MESH)

    def x_arrival(step, part):
        place = far.at[0, away, step] if part == 0 else far.at[0, near, step, 1 - x_lo]
        return pltpu.make_async_remote_copy(place, place, s_x.at[part, step], r_x.at[part, step], across, MESH)

    def pair_copy(step, which, send):
        if which == 1:
            place = far.at[1, near if send else away, step, x_lo if send else 1 - x_lo]
        else:
            place = far.at[0, away if send else near, step, 1 - x_lo if send else x_lo]
        return pltpu.make_async_remote_copy(place, place, s_f.at[which, step], r_f.at[which, step], pair_near, MESH)

    def send_own(step):
        for copy in own_copies(step):
            copy.start()

    def stage_own(step):
        arrivals = own_arrivals(step)
        arrivals[2].wait_recv()

        @pl.when(jnp.logical_and(step == 0, jnp.logical_not(late)))
        def _():
            pl.semaphore_wait(z_ready, 1)

        @pl.when(jnp.logical_not(late))
        def _():
            z_copy(step, 0).start()

        @pl.when(x_hi == 1)
        def _():
            x_copy(step, 0, False).start()

        arrivals[0].wait_recv()
        arrivals[1].wait_recv()

        @pl.when(jnp.logical_not(late))
        def _():
            z_copy(step, 1).start()

        @pl.when(x_hi == 1)
        def _():
            x_copy(step, 1, False).start()

    def stage_z(step):
        z_copy(step, 0).wait_recv()
        pair_copy(step, 1, True).start()

        @pl.when(x_hi == 0)
        def _():
            x_copy(step, 0, True).start()

        z_copy(step, 1).wait_recv()

        @pl.when(x_hi == 0)
        def _():
            x_copy(step, 1, True).start()

    def stage_x(step):
        x_arrival(step, 0).wait_recv()
        pair_copy(step, 0, True).start()
        x_arrival(step, 1).wait_recv()

    lane = lax.broadcasted_iota(jnp.int32, (8, 128), 1)
    row = lax.broadcasted_iota(jnp.int32, (8, 128), 0)
    low_lanes = lax.broadcasted_iota(jnp.int32, (256, CB), 1) < HALF
    mask = (lax.rem(lane, 8) == row).astype(jnp.float32)

    def spectrum(step, k):
        if k == 0:
            for part in range(2):
                rows = pl.ds(part * 32, 32)
                picked = jnp.concatenate([own[s, step, x_lo, rows, :] for s in range(SEGS)], 0)
                turned[part] = picked.astype(jnp.float32).T
        base = ROWS * lax.rem(k + x_lo, 2)
        for i in range(ROWS):
            u = turned[0, pl.ds(base + i, 1), :] * mask
            v = turned[1, pl.ds(base + i, 1), :] * mask
            left[pl.ds(i * 16, 16), 0:128] = jnp.concatenate([u, v], 0).astype(jnp.bfloat16)
            left[pl.ds(i * 16, 16), 128:256] = jnp.concatenate([v, -u], 0).astype(jnp.bfloat16)
        blocks = []
        for r in range(ROUNDS):
            low, high = [
                jnp.concatenate(
                    [far[r, s, step, half, pl.ds(part * 32, 32), :] for part in range(2) for s in range(SEGS)], 0
                ).astype(jnp.float32)
                for half in range(2)
            ]
            if k == 0:
                block = jnp.where(low_lanes, low, high)
            else:
                block = pltpu.roll(jnp.where(low_lanes, high, low), HALF, 1)
            blocks.append(block.astype(jnp.bfloat16))
        right = jnp.concatenate(blocks, 1)
        product = jnp.dot(left[...], right, preferred_element_type=jnp.float32)
        group = step * PER_STEP + k
        spot = pl.multiple_of(lax.rem(group, BURST) * 16, 16)
        slot = lax.rem(group // BURST, 2)
        cross[slot, :, pl.ds(spot, 16), :] = product.reshape(ROWS, 16, ROUNDS * CB).astype(jnp.bfloat16)

    def projected(burst, i):
        columns = pl.ds(pl.multiple_of(burst * BURST * 16, BURST * 16), BURST * 16)
        slot = burst % 2 if isinstance(burst, int) else lax.rem(burst, 2)
        return jnp.dot(table[:, columns], cross[slot, i], preferred_element_type=jnp.float32)

    per_burst = BURST // PER_STEP
    share = ROWS // per_burst

    def project_share(step):
        burst = step // per_burst - 1
        first = lax.rem(step, per_burst) * share

        @pl.when(burst == 0)
        def _():
            for k in range(share):
                acc[first + k] = projected(burst, first + k)

        @pl.when(burst > 0)
        def _():
            for k in range(share):
                acc[first + k] = acc[first + k] + projected(burst, first + k)

    prepare(0)
    prepare(2)
    pl.semaphore_wait(barrier, 5)
    pl.semaphore_signal(z_ready, inc=1, device_id=above, device_id_type=MESH)
    for step in range(AHEAD):
        send_own(step)
    prepare(1)
    prepare(3)
    table_copy.wait()

    @pl.loop(0, STEPS + LAG_C)
    def _(t):
        @pl.when(t + AHEAD < STEPS)
        def _():
            send_own(t + AHEAD)

        @pl.when(t < STEPS)
        def _():
            stage_own(t)

        @pl.when(jnp.logical_and(late, t == Z_DELAY))
        def _():
            pl.semaphore_wait(z_ready, 1)

        @pl.when(jnp.logical_and(late, jnp.logical_and(t >= Z_DELAY, t < STEPS + Z_DELAY)))
        def _():
            z_copy(t - Z_DELAY, 0).start()
            z_copy(t - Z_DELAY, 1).start()

        @pl.when(t >= LAG_C)
        def _():
            pair_copy(t - LAG_C, 1, False).wait_recv()
            pair_copy(t - LAG_C, 0, False).wait_recv()
            spectrum(t - LAG_C, 0)

        @pl.when(jnp.logical_and(t >= LAG_F2, t < STEPS + LAG_F2))
        def _():
            stage_z(t - LAG_F2)

        @pl.when(t >= LAG_C)
        def _():
            spectrum(t - LAG_C, 1)

        @pl.when(jnp.logical_and(t >= LAG_F1, t < STEPS + LAG_F1))
        def _():
            stage_x(t - LAG_F1)

        @pl.when(t >= LAG_C + per_burst)
        def _():
            project_share(t - LAG_C)

    per_piece = OUT_ROWS // PIECES
    last = GROUPS // BURST - 1

    def sum_copy(piece):
        rows = pl.ds(piece * per_piece, per_piece)
        return pltpu.make_async_remote_copy(
            sums.at[rows], landed.at[rows], s_sum.at[piece], r_sum.at[piece], sibling, MESH)

    for piece in range(PIECES):
        for k in range(per_piece):
            q = piece * per_piece + k
            i = (1 - core) * OUT_ROWS + q
            sums[q] = (acc[i] + projected(last, i)).astype(jnp.bfloat16)
        sum_copy(piece).start()

    @pl.loop(0, OUT_ROWS // UNROLL)
    def _(first):
        for k in range(UNROLL):
            q = first * UNROLL + k
            i = core * OUT_ROWS + q
            kept[q] = acc[i] + projected(last, i)

    for piece in range(PIECES):
        sum_copy(piece).wait_recv()

    @pl.loop(0, STEPS)
    def _(step):
        for copy in own_copies(step):
            copy.wait_send()

        for part in range(2):
            z_copy(step, part).wait_send()
            x_copy(step, part, False).wait_send()
            pair_copy(step, part, True).wait_send()

    for piece in range(PIECES):
        sum_copy(piece).wait_send()


def finish(kept, landed, out, turned, sems):
    scale = 1.0 / math.sqrt(F * SEGS)
    blocks = LAG_ROWS // LAG_BLOCK
    block_rows = LAG_BLOCK * OUT_ROWS
    last_rows = LAGS * OUT_ROWS - (blocks - 1) * block_rows

    def leave(n, act):
        r, block = n // blocks, lax.rem(n, blocks)
        for rows, here in ((block_rows, block < blocks - 1), (last_rows, block == blocks - 1)):
            @pl.when(here)
            def _():
                start = pl.multiple_of(block * block_rows, 8)
                act(pltpu.make_async_copy(turned.at[n, pl.ds(0, rows)], out.at[r, pl.ds(start, rows)], sems.at[n]))

    @pl.loop(0, ROUNDS * blocks)
    def _(n):
        lanes = pl.ds(pl.multiple_of(n // blocks * CB, CB), CB)
        lags = pl.ds(pl.multiple_of(lax.rem(n, blocks) * LAG_BLOCK, LAG_BLOCK), LAG_BLOCK)
        for i in range(0, OUT_ROWS, 8):
            rows = pl.ds(i, 8)
            total = (kept[rows, lags, lanes] + landed[rows, lags, lanes].astype(jnp.float32)) * scale
            total = jnp.swapaxes(total, 0, 1)
            for lag in range(LAG_BLOCK):
                turned[n, pl.ds(lag * OUT_ROWS + i, 8), :] = total[lag]
        leave(n, lambda copy: copy.start())

    @pl.loop(0, ROUNDS * blocks)
    def _(n):
        leave(n, lambda copy: copy.wait())


def local(n_chan, table, spectra, valid):
    kept, landed = pl.pallas_call(
        functools.partial(kernel, n_chan),
        name="correlate",
        out_shape=[
            pltpu.VMEM((OUT_ROWS, LAG_ROWS, ROUNDS * CB), jnp.float32),
            pltpu.VMEM((OUT_ROWS, LAG_ROWS, ROUNDS * CB), jnp.bfloat16),
        ],
        in_specs=[
            pl.BlockSpec(memory_space=pltpu.HBM),
            pl.BlockSpec(memory_space=pltpu.HBM),
            pl.BlockSpec(memory_space=pltpu.HBM),
        ],
        out_specs=[pl.BlockSpec(memory_space=pltpu.VMEM)] * 2,
        scratch_shapes=[
            pltpu.VMEM((1, CB), jnp.int32),
            pltpu.VMEM((LAG_ROWS, GROUPS * 16), jnp.bfloat16),
            pltpu.VMEM((4, 2, WIN, CB, 128), jnp.float32),
            pltpu.VMEM((SEGS, STEPS, 2, 64, CB), jnp.bfloat16),
            pltpu.VMEM((ROUNDS, SEGS, STEPS, 2, 64, CB), jnp.bfloat16),
            pltpu.VMEM((STEPS, 2, 64, CB), jnp.bfloat16),
            pltpu.VMEM((2, CB, 128), jnp.float32),
            pltpu.VMEM((ROWS * 16, 256), jnp.bfloat16),
            pltpu.VMEM((2, ROWS, BURST * 16, ROUNDS * CB), jnp.bfloat16),
            pltpu.VMEM((ROWS, LAG_ROWS, ROUNDS * CB), jnp.float32),
            pltpu.VMEM((OUT_ROWS, LAG_ROWS, ROUNDS * CB), jnp.bfloat16),
            pltpu.SemaphoreType.DMA((4, 2)),
            pltpu.SemaphoreType.DMA((2,)),
            pltpu.SemaphoreType.DMA((3, STEPS)),
            pltpu.SemaphoreType.DMA((3, STEPS)),
            pltpu.SemaphoreType.DMA((2, STEPS)),
            pltpu.SemaphoreType.DMA((2, STEPS)),
            pltpu.SemaphoreType.DMA((2, STEPS)),
            pltpu.SemaphoreType.DMA((2, STEPS)),
            pltpu.SemaphoreType.DMA((2, STEPS)),
            pltpu.SemaphoreType.DMA((2, STEPS)),
            pltpu.SemaphoreType.DMA((PIECES,)),
            pltpu.SemaphoreType.DMA((PIECES,)),
            pltpu.SemaphoreType.REGULAR,
        ],
        compiler_params=pltpu.CompilerParams(
            collective_id=0, has_side_effects=True, vmem_limit_bytes=32 * 2**20),
    )(*(pltpu.with_memory_space_constraint(x, pltpu.HBM) for x in (spectra, valid, table)))
    in_vmem = pl.BlockSpec(memory_space=pltpu.VMEM)
    stacked = pl.pallas_call(
        finish,
        name="finish",
        out_shape=jax.ShapeDtypeStruct((ROUNDS, LAGS * OUT_ROWS, CB), jnp.float32),
        in_specs=[in_vmem, in_vmem],
        out_specs=pl.BlockSpec(memory_space=pltpu.HBM),
        scratch_shapes=[
            pltpu.VMEM((ROUNDS * (LAG_ROWS // LAG_BLOCK), LAG_BLOCK * OUT_ROWS, CB), jnp.float32),
            pltpu.SemaphoreType.DMA((ROUNDS * (LAG_ROWS // LAG_BLOCK),)),
        ],
        compiler_params=pltpu.CompilerParams(vmem_limit_bytes=16 * 2**20),
    )(pltpu.with_memory_space_constraint(kept, pltpu.VMEM), pltpu.with_memory_space_constraint(landed, pltpu.VMEM))
    return stacked.reshape(ROUNDS, 1, LAGS, OUT_ROWS, CB).transpose(0, 1, 3, 2, 4)


def solution(mesh):
    n_chan = mesh.shape["chan"]

    def run(spectra, valid):
        table = jnp.asarray(np.stack([lag_table(0), lag_table(1)]).astype(ml_dtypes.bfloat16))
        return jax.shard_map(
            functools.partial(local, n_chan, table),
            mesh=mesh,
            in_specs=(P("seg", None, "chan", None), P("seg", "chan")),
            out_specs=P(None, "chan", "seg", None, None),
            check_vma=False,
        )(spectra, valid)

    return run
```

```python
import functools
import math

import jax
import jax.numpy as jnp
import ml_dtypes
import numpy as np
from jax import lax
from jax.experimental import pallas as pl
from jax.experimental.pallas import tpu as pltpu
from jax.sharding import PartitionSpec as P

MESH = pl.DeviceIdType.MESH
ROUNDS = 2
LAGS = 101
LAG_ROWS = 112
SEGS = 4
WIN = 4
CB = 128
F = 512
HALF_F = F // 2
GROUPS = HALF_F // 8
PER_STEP = 2
STEPS = GROUPS // PER_STEP
BURST = 8
ROWS = CB // 2
OUT_ROWS = CB // SEGS
HALF = CB // 2
AHEAD = 2
LAG_F2 = 2
LAG_F1 = 3
LAG_C = 5
Z_SIZE = 8
Z_DELAY = 1
PIECES = 4
LAG_BLOCK = 16
UNROLL = 8


def lag_table(core):
    f = core * HALF_F + np.arange(HALF_F, dtype=np.int64).reshape(GROUPS, 1, 8)
    t = np.arange(LAGS, dtype=np.int64).reshape(LAGS, 1, 1, 1) - (LAGS - 1) // 2
    phase = np.mod(f * t, 2 * F) * (math.pi / F)
    both = np.concatenate([np.cos(phase), -np.sin(phase)], 2).reshape(LAGS, GROUPS * 16)
    return np.pad(both, ((0, LAG_ROWS - LAGS), (0, 0)))


def kernel(n_chan, spectra, valid_in, table_in, kept, landed, valid, table, staged, own, far, other, turned, left, cross, acc, sums,
           in_sem, small_sem, s_own, r_own, s_z, r_z, s_x, r_x, s_f, r_f, s_sum, r_sum, z_ready):
    seg = lax.axis_index("seg")
    chan = lax.axis_index("chan")
    core = lax.rem(seg, 2)
    x_lo = seg // 2
    x_hi = lax.rem(chan, 2)
    sibling = (seg + 1 - 2 * core, chan)
    pair_near = (lax.rem(seg + 2, SEGS), chan)
    pair_cross = (SEGS - 1 - seg, chan)
    below = (seg, lax.rem(chan + n_chan - 2, n_chan))
    above = (seg, lax.rem(chan + 2, n_chan))
    across = (lax.rem(seg + 2, SEGS), chan + 1 - 2 * x_hi)
    near = pl.ds(2 * x_lo, 2)
    away = pl.ds(2 - 2 * x_lo, 2)

    barrier = pltpu.get_barrier_semaphore()
    late = lax.rem(chan // 2, Z_SIZE) == 0
    for device in (sibling, pair_near, pair_cross, below, across):
        pl.semaphore_signal(barrier, inc=1, device_id=device, device_id_type=MESH)

    def load(block):
        half = lax.rem(core + block // 2, 2)
        first = half * HALF_F + lax.rem(block, 2) * 128
        copies = []
        for part in range(2):
            source = pl.multiple_of(first + part * F, 128)
            copies.append(pltpu.make_async_copy(
                spectra.at[0, :, :, pl.ds(source, 128)],
                staged.at[block, part],
                in_sem.at[block, part],
            ))
        return copies

    valid_copy = pltpu.make_async_copy(valid_in, valid, small_sem.at[0])
    table_copy = pltpu.make_async_copy(table_in.at[core], table, small_sem.at[1])
    valid_copy.start()
    for block in (0, 2, 1, 3):
        for copy in load(block):
            copy.start()

    table_copy.start()
    valid_copy.wait()
    first_half = lax.broadcasted_iota(jnp.int32, (8, 8, CB), 2) < HALF
    counts = valid[...]
    inverse = 1.0 / jnp.sqrt(counts.astype(jnp.float32))
    weights = [jnp.where(w < counts, inverse, 0.0) for w in range(WIN)]

    def prepare(block):
        for copy in load(block):
            copy.wait()
        steps = pl.ds(8 * (block % 2), 8)
        for part in range(2):
            for pair in range(2):
                lows, highs = [], []
                for w in (2 * pair, 2 * pair + 1):
                    rows = (staged[block, part, w].T * weights[w]).reshape(8, 2, 8, CB)
                    even = rows[:, 0]
                    odd = pltpu.roll(rows[:, 1].reshape(64, CB), HALF, 1).reshape(8, 8, CB)
                    lows.append(jnp.where(first_half, even, odd))
                    highs.append(jnp.where(first_half, odd, even))
                place = pl.ds(part * 32 + pair * 16, 16)
                for half, both in enumerate((lows, highs)):
                    both = jnp.concatenate(both, 1).astype(jnp.bfloat16)
                    if block < 2:
                        own[seg, steps, half, place, :] = both
                    else:
                        other[steps, half, place, :] = both

    def own_copies(step):
        half = 1 - x_lo
        target = own.at[seg, step, half]
        return [
            pltpu.make_async_remote_copy(
                own.at[seg, step, half], target, s_own.at[0, step], r_own.at[0, step], pair_near, MESH),
            pltpu.make_async_remote_copy(
                other.at[step, half], target, s_own.at[1, step], r_own.at[1, step], pair_cross, MESH),
            pltpu.make_async_remote_copy(
                other.at[step], own.at[seg, step], s_own.at[2, step], r_own.at[2, step], sibling, MESH),
        ]

    def own_arrivals(step):
        def arrival(kind, place):
            return pltpu.make_async_remote_copy(
                place, place, s_own.at[kind, step], r_own.at[kind, step], sibling, MESH)

        return [
            arrival(0, own.at[pair_near[0], step, x_lo]),
            arrival(1, own.at[pair_cross[0], step, x_lo]),
            arrival(2, own.at[sibling[0], step]),
        ]

    def z_copy(step, part):
        if part == 0:
            source, target = own.at[near, step], far.at[1, near, step]
        else:
            source, target = own.at[away, step, x_lo], far.at[1, away, step, x_lo]
        return pltpu.make_async_remote_copy(source, target, s_z.at[part, step], r_z.at[part, step], below, MESH)

    def x_copy(step, part, from_far):
        segs = near if part == 0 else away
        place = (segs, step) if part == 0 else (segs, step, x_lo)
        source = far.at[(1,) + place] if from_far else own.at[place]
        return pltpu.make_async_remote_copy(
            source, far.at[(0,) + place], s_x.at[part, step], r_x.at[part, step], across, MESH)

    def x_arrival(step, part):
        place = far.at[0, away, step] if part == 0 else far.at[0, near, step, 1 - x_lo]
        return pltpu.make_async_remote_copy(place, place, s_x.at[part, step], r_x.at[part, step], across, MESH)

    def pair_copy(step, which, send):
        if which == 1:
            place = far.at[1, near if send else away, step, x_lo if send else 1 - x_lo]
        else:
            place = far.at[0, away if send else near, step, 1 - x_lo if send else x_lo]
        return pltpu.make_async_remote_copy(place, place, s_f.at[which, step], r_f.at[which, step], pair_near, MESH)

    def send_own(step):
        for copy in own_copies(step):
            copy.start()

    def stage_own(step):
        arrivals = own_arrivals(step)
        arrivals[2].wait_recv()

        @pl.when(jnp.logical_and(step == 0, jnp.logical_not(late)))
        def _():
            pl.semaphore_wait(z_ready, 1)

        @pl.when(jnp.logical_not(late))
        def _():
            z_copy(step, 0).start()

        @pl.when(x_hi == 1)
        def _():
            x_copy(step, 0, False).start()

        arrivals[0].wait_recv()
        arrivals[1].wait_recv()

        @pl.when(jnp.logical_not(late))
        def _():
            z_copy(step, 1).start()

        @pl.when(x_hi == 1)
        def _():
            x_copy(step, 1, False).start()

    def stage_z(step):
        z_copy(step, 0).wait_recv()
        pair_copy(step, 1, True).start()

        @pl.when(x_hi == 0)
        def _():
            x_copy(step, 0, True).start()

        z_copy(step, 1).wait_recv()

        @pl.when(x_hi == 0)
        def _():
            x_copy(step, 1, True).start()

    def stage_x(step):
        x_arrival(step, 0).wait_recv()
        pair_copy(step, 0, True).start()
        x_arrival(step, 1).wait_recv()

    lane = lax.broadcasted_iota(jnp.int32, (8, 128), 1)
    row = lax.broadcasted_iota(jnp.int32, (8, 128), 0)
    low_lanes = lax.broadcasted_iota(jnp.int32, (256, CB), 1) < HALF
    mask = (lax.rem(lane, 8) == row).astype(jnp.float32)

    def spectrum(step, k):
        if k == 0:
            for part in range(2):
                rows = pl.ds(part * 32, 32)
                picked = jnp.concatenate([own[s, step, x_lo, rows, :] for s in range(SEGS)], 0)
                turned[part] = picked.astype(jnp.float32).T
        base = ROWS * lax.rem(k + x_lo, 2)
        for i in range(ROWS):
            u = turned[0, pl.ds(base + i, 1), :] * mask
            v = turned[1, pl.ds(base + i, 1), :] * mask
            left[pl.ds(i * 16, 16), 0:128] = jnp.concatenate([u, v], 0).astype(jnp.bfloat16)
            left[pl.ds(i * 16, 16), 128:256] = jnp.concatenate([v, -u], 0).astype(jnp.bfloat16)
        blocks = []
        for r in range(ROUNDS):
            low, high = [
                jnp.concatenate(
                    [far[r, s, step, half, pl.ds(part * 32, 32), :] for part in range(2) for s in range(SEGS)], 0
                ).astype(jnp.float32)
                for half in range(2)
            ]
            if k == 0:
                block = jnp.where(low_lanes, low, high)
            else:
                block = pltpu.roll(jnp.where(low_lanes, high, low), HALF, 1)
            blocks.append(block.astype(jnp.bfloat16))
        right = jnp.concatenate(blocks, 1)
        product = jnp.dot(left[...], right, preferred_element_type=jnp.float32)
        group = step * PER_STEP + k
        spot = pl.multiple_of(lax.rem(group, BURST) * 16, 16)
        slot = lax.rem(group // BURST, 2)
        cross[slot, :, pl.ds(spot, 16), :] = product.reshape(ROWS, 16, ROUNDS * CB).astype(jnp.bfloat16)

    def projected(burst, i):
        columns = pl.ds(pl.multiple_of(burst * BURST * 16, BURST * 16), BURST * 16)
        slot = burst % 2 if isinstance(burst, int) else lax.rem(burst, 2)
        return jnp.dot(table[:, columns], cross[slot, i], preferred_element_type=jnp.float32)

    per_burst = BURST // PER_STEP
    share = ROWS // per_burst

    def project_share(step):
        burst = step // per_burst - 1
        first = lax.rem(step, per_burst) * share

        @pl.when(burst == 0)
        def _():
            for k in range(share):
                acc[first + k] = projected(burst, first + k)

        @pl.when(burst > 0)
        def _():
            for k in range(share):
                acc[first + k] = acc[first + k] + projected(burst, first + k)

    prepare(0)
    prepare(2)
    pl.semaphore_wait(barrier, 5)
    pl.semaphore_signal(z_ready, inc=1, device_id=above, device_id_type=MESH)
    for step in range(AHEAD):
        send_own(step)
    prepare(1)
    prepare(3)
    table_copy.wait()

    @pl.loop(0, STEPS + LAG_C)
    def _(t):
        @pl.when(t + AHEAD < STEPS)
        def _():
            send_own(t + AHEAD)

        @pl.when(jnp.logical_and(late, t == Z_DELAY))
        def _():
            pl.semaphore_wait(z_ready, 1)

        @pl.when(jnp.logical_and(late, jnp.logical_and(t >= Z_DELAY, t < STEPS + Z_DELAY)))
        def _():
            z_copy(t - Z_DELAY, 0).start()
            z_copy(t - Z_DELAY, 1).start()

        @pl.when(t < STEPS)
        def _():
            stage_own(t)

        @pl.when(t >= LAG_C)
        def _():
            pair_copy(t - LAG_C, 1, False).wait_recv()
            pair_copy(t - LAG_C, 0, False).wait_recv()
            spectrum(t - LAG_C, 0)

        @pl.when(jnp.logical_and(t >= LAG_F2, t < STEPS + LAG_F2))
        def _():
            stage_z(t - LAG_F2)

        @pl.when(t >= LAG_C)
        def _():
            spectrum(t - LAG_C, 1)

        @pl.when(jnp.logical_and(t >= LAG_F1, t < STEPS + LAG_F1))
        def _():
            stage_x(t - LAG_F1)

        @pl.when(t >= LAG_C + per_burst)
        def _():
            project_share(t - LAG_C)

    per_piece = OUT_ROWS // PIECES
    last = GROUPS // BURST - 1

    def sum_copy(piece):
        rows = pl.ds(piece * per_piece, per_piece)
        return pltpu.make_async_remote_copy(
            sums.at[rows], landed.at[rows], s_sum.at[piece], r_sum.at[piece], sibling, MESH)

    for piece in range(PIECES):
        for k in range(per_piece):
            q = piece * per_piece + k
            i = (1 - core) * OUT_ROWS + q
            sums[q] = (acc[i] + projected(last, i)).astype(jnp.bfloat16)
        sum_copy(piece).start()

    @pl.loop(0, OUT_ROWS // UNROLL)
    def _(first):
        for k in range(UNROLL):
            q = first * UNROLL + k
            i = core * OUT_ROWS + q
            kept[q] = acc[i] + projected(last, i)

    for piece in range(PIECES):
        sum_copy(piece).wait_recv()

    @pl.loop(0, STEPS)
    def _(step):
        for copy in own_copies(step):
            copy.wait_send()

        for part in range(2):
            z_copy(step, part).wait_send()
            x_copy(step, part, False).wait_send()
            pair_copy(step, part, True).wait_send()

    for piece in range(PIECES):
        sum_copy(piece).wait_send()


def finish(kept, landed, out, turned, sems):
    scale = 1.0 / math.sqrt(F * SEGS)
    blocks = LAG_ROWS // LAG_BLOCK
    block_rows = LAG_BLOCK * OUT_ROWS
    last_rows = LAGS * OUT_ROWS - (blocks - 1) * block_rows

    def leave(n, act):
        r, block = n // blocks, lax.rem(n, blocks)
        for rows, here in ((block_rows, block < blocks - 1), (last_rows, block == blocks - 1)):
            @pl.when(here)
            def _():
                start = pl.multiple_of(block * block_rows, 8)
                act(pltpu.make_async_copy(turned.at[n, pl.ds(0, rows)], out.at[r, pl.ds(start, rows)], sems.at[n]))

    @pl.loop(0, ROUNDS * blocks)
    def _(n):
        lanes = pl.ds(pl.multiple_of(n // blocks * CB, CB), CB)
        lags = pl.ds(pl.multiple_of(lax.rem(n, blocks) * LAG_BLOCK, LAG_BLOCK), LAG_BLOCK)
        for i in range(0, OUT_ROWS, 8):
            rows = pl.ds(i, 8)
            total = (kept[rows, lags, lanes] + landed[rows, lags, lanes].astype(jnp.float32)) * scale
            total = jnp.swapaxes(total, 0, 1)
            for lag in range(LAG_BLOCK):
                turned[n, pl.ds(lag * OUT_ROWS + i, 8), :] = total[lag]
        leave(n, lambda copy: copy.start())

    @pl.loop(0, ROUNDS * blocks)
    def _(n):
        leave(n, lambda copy: copy.wait())


def local(n_chan, table, spectra, valid):
    kept, landed = pl.pallas_call(
        functools.partial(kernel, n_chan),
        name="correlate",
        out_shape=[
            pltpu.VMEM((OUT_ROWS, LAG_ROWS, ROUNDS * CB), jnp.float32),
            pltpu.VMEM((OUT_ROWS, LAG_ROWS, ROUNDS * CB), jnp.bfloat16),
        ],
        in_specs=[
            pl.BlockSpec(memory_space=pltpu.HBM),
            pl.BlockSpec(memory_space=pltpu.HBM),
            pl.BlockSpec(memory_space=pltpu.HBM),
        ],
        out_specs=[pl.BlockSpec(memory_space=pltpu.VMEM)] * 2,
        scratch_shapes=[
            pltpu.VMEM((1, CB), jnp.int32),
            pltpu.VMEM((LAG_ROWS, GROUPS * 16), jnp.bfloat16),
            pltpu.VMEM((4, 2, WIN, CB, 128), jnp.float32),
            pltpu.VMEM((SEGS, STEPS, 2, 64, CB), jnp.bfloat16),
            pltpu.VMEM((ROUNDS, SEGS, STEPS, 2, 64, CB), jnp.bfloat16),
            pltpu.VMEM((STEPS, 2, 64, CB), jnp.bfloat16),
            pltpu.VMEM((2, CB, 128), jnp.float32),
            pltpu.VMEM((ROWS * 16, 256), jnp.bfloat16),
            pltpu.VMEM((2, ROWS, BURST * 16, ROUNDS * CB), jnp.bfloat16),
            pltpu.VMEM((ROWS, LAG_ROWS, ROUNDS * CB), jnp.float32),
            pltpu.VMEM((OUT_ROWS, LAG_ROWS, ROUNDS * CB), jnp.bfloat16),
            pltpu.SemaphoreType.DMA((4, 2)),
            pltpu.SemaphoreType.DMA((2,)),
            pltpu.SemaphoreType.DMA((3, STEPS)),
            pltpu.SemaphoreType.DMA((3, STEPS)),
            pltpu.SemaphoreType.DMA((2, STEPS)),
            pltpu.SemaphoreType.DMA((2, STEPS)),
            pltpu.SemaphoreType.DMA((2, STEPS)),
            pltpu.SemaphoreType.DMA((2, STEPS)),
            pltpu.SemaphoreType.DMA((2, STEPS)),
            pltpu.SemaphoreType.DMA((2, STEPS)),
            pltpu.SemaphoreType.DMA((PIECES,)),
            pltpu.SemaphoreType.DMA((PIECES,)),
            pltpu.SemaphoreType.REGULAR,
        ],
        compiler_params=pltpu.CompilerParams(
            collective_id=0, has_side_effects=True, vmem_limit_bytes=32 * 2**20),
    )(*(pltpu.with_memory_space_constraint(x, pltpu.HBM) for x in (spectra, valid, table)))
    in_vmem = pl.BlockSpec(memory_space=pltpu.VMEM)
    stacked = pl.pallas_call(
        finish,
        name="finish",
        out_shape=jax.ShapeDtypeStruct((ROUNDS, LAGS * OUT_ROWS, CB), jnp.float32),
        in_specs=[in_vmem, in_vmem],
        out_specs=pl.BlockSpec(memory_space=pltpu.HBM),
        scratch_shapes=[
            pltpu.VMEM((ROUNDS * (LAG_ROWS // LAG_BLOCK), LAG_BLOCK * OUT_ROWS, CB), jnp.float32),
            pltpu.SemaphoreType.DMA((ROUNDS * (LAG_ROWS // LAG_BLOCK),)),
        ],
        compiler_params=pltpu.CompilerParams(vmem_limit_bytes=16 * 2**20),
    )(pltpu.with_memory_space_constraint(kept, pltpu.VMEM), pltpu.with_memory_space_constraint(landed, pltpu.VMEM))
    return stacked.reshape(ROUNDS, 1, LAGS, OUT_ROWS, CB).transpose(0, 1, 3, 2, 4)


def solution(mesh):
    n_chan = mesh.shape["chan"]

    def run(spectra, valid):
        table = jnp.asarray(np.stack([lag_table(0), lag_table(1)]).astype(ml_dtypes.bfloat16))
        return jax.shard_map(
            functools.partial(local, n_chan, table),
            mesh=mesh,
            in_specs=(P("seg", None, "chan", None), P("seg", "chan")),
            out_specs=P(None, "chan", "seg", None, None),
            check_vma=False,
        )(spectra, valid)

    return run
```
